128 devices in a mesh: row: 8 (over y, x_hi), col: 16 (over z, x_lo, core).
Axes of the slice: x: 4 (x_hi: 2, x_lo: 2; x = x_hi * 2 + x_lo), y: 4, z: 4, core: 2. Of those that a mesh axis runs over, the one named last changes fastest.
Arguments:
- amplitudes: bfloat16 [4096, 16384], P('col', 'row'), may hold values from -6 to 6
- integrals: bfloat16 [4096, 16384], P('row', 'col'), may hold values from -0.09375 to 0.09375
- tile_mask: int32 [64, 256], P(None, 'row'), may hold values from 0 to 1, as said below
- occ_energy: float32 [4], replicated, may hold values from -1 to -0.2
- virt_energy: float32 [4096], replicated, may hold values from 0.2 to 1.5
Outputs:
- update: bfloat16 [16384, 16384], P(('row', 'col'))
The draws below stay inside these ranges and needn't reach their ends.
Inputs may be any that keep to these rules, and one draw needn't show every extreme that they name: `tile_mask`: 0 drops a tile, 1 keeps it; the share of kept tiles differs strongly between groups of (ia) rows.
All inputs are finite; a program needn't handle non-finite values.
Results may differ from the reference program's by a relative error of at most 0.0049.
Values may be sent and summed in bfloat16 or wider, within the bound.
No kernel may reach another device: no remote copies, remote signals or barrier semaphores. Data moves between devices by JAX's collectives and lax.ppermute only.
A program may use at most 128 MiB of HBM per device.

```python
import jax
import jax.numpy as jnp
from jax import lax

V = 4096
TILE = 64
NI = 4
KW = 4096
M = 16384
N_ROW = 8
N_COL = 16


def draw_tile_mask(key, part):
    tile_depth = KW // TILE
    tile_width = M // TILE
    groups = N_ROW
    depth_blocks = N_COL
    first_key, second_key = jax.random.split(jax.random.fold_in(key, 7))
    levels = jax.random.randint(first_key, (depth_blocks, groups), 0, 100)
    bounds = 20 + 70 * jnp.arange(groups, dtype=jnp.int32) // max(groups - 1, 1)
    active = (levels < bounds[None, :]).astype(jnp.int32)
    active = jnp.repeat(jnp.repeat(active, tile_depth // depth_blocks, axis=0), tile_width // groups, axis=1)
    tiles = (jax.random.randint(second_key, (tile_depth, tile_width), 0, 4) > 0).astype(jnp.int32)
    return active * tiles


def block_scale(rng, shape, cuts, least, top_value):
    loudness = 1.0
    for dim, parts in cuts:
        steps = jax.random.uniform(jax.random.fold_in(jax.random.fold_in(rng, 6), dim), (parts,), jnp.float32, least / len(cuts), top_value / len(cuts))
        loudness = loudness * jnp.repeat(jnp.exp(steps), shape[dim] // parts).reshape((-1,) + (1,) * (len(shape) - 1 - dim))
    return loudness


def noise(rng, extent, spread, most, pieces=(), kind=jnp.bfloat16):
    level = block_scale(rng, extent, pieces, -0.22, 0.18) if pieces else 1.0
    values = jax.random.normal(rng, extent, jnp.float32) * spread * level
    return jnp.minimum(jnp.maximum(values, -most), most).astype(kind)


def setup_inputs(seed: int = 0) -> dict:
    key_list = jax.random.split(jax.random.key(seed), 6)
    return {
        "amplitudes": noise(key_list[0], (KW, M), 1.0, 6.0, ((0, 16), (1, 8))),
        "integrals": noise(key_list[1], (KW, M), KW ** -0.5, 0.09375, ((0, 8), (1, 16))),
        "tile_mask": draw_tile_mask(jax.random.fold_in(key_list[5], 71), 0),
        "occ_energy": jnp.clip(jax.random.uniform(key_list[3], (NI,), jnp.float32, -1.0, -0.2), -1.0, -0.2),
        "virt_energy": jnp.clip(jax.random.uniform(key_list[4], (V,), jnp.float32, 0.2, 1.5), 0.2, 1.5),
    }


def reference(amplitudes, integrals, tile_mask, occ_energy, virt_energy):
    tile_depth, tile_width = tile_mask.shape
    keep_tiles = tile_mask.astype(jnp.bfloat16)
    masked = (amplitudes.reshape(tile_depth, TILE, tile_width, TILE) * keep_tiles[:, None, :, None]).reshape(KW, M)
    cycle_block = jnp.dot(masked.T, integrals, preferred_element_type=jnp.float32).astype(jnp.bfloat16)
    pair_gap = (virt_energy[None, :] - occ_energy[:, None]).astype(jnp.float32).reshape(M)
    block_rows = min(M, 1024)

    def mirror_block(index_block):
        offset = index_block * block_rows
        row_block = lax.dynamic_slice_in_dim(cycle_block, offset, block_rows, 0).astype(jnp.float32)
        col_block = lax.dynamic_slice_in_dim(cycle_block, offset, block_rows, 1).astype(jnp.float32).T
        gap_block = lax.dynamic_slice_in_dim(pair_gap, offset, block_rows, 0)
        return ((row_block + col_block) / (gap_block[:, None] + pair_gap[None, :])).astype(jnp.bfloat16)

    result = lax.map(mirror_block, jnp.arange(M // block_rows, dtype=jnp.int32))
    return result.reshape(M, M)
```

```python
import functools

import jax
import jax.numpy as jnp
from jax import lax
from jax.experimental import pallas as pl
from jax.experimental.pallas import tpu as pltpu
from jax.sharding import PartitionSpec as P

TILE = 64
CHUNKS = 2
BF = jnp.bfloat16
F32 = jnp.float32


def col_pairs(move):
    pairs = []
    for z in range(4):
        for x in range(2):
            for k in range(2):
                a, b, c = move(z, x, k)
                pairs.append((z * 4 + x * 2 + k, (a % 4) * 4 + (b % 2) * 2 + c % 2))
    return pairs


def row_pairs(move):
    pairs = []
    for y in range(4):
        for x in range(2):
            a, b = move(y, x)
            pairs.append((y * 2 + x, (a % 4) * 2 + b % 2))
    return pairs


Z_UP = col_pairs(lambda z, x, k: (z + 1, x, k))
Z_DOWN = col_pairs(lambda z, x, k: (z - 1, x, k))
X_SWAP = col_pairs(lambda z, x, k: (z, x + 1, k))
CORE_SWAP = col_pairs(lambda z, x, k: (z, x, k + 1))
Y_UP = row_pairs(lambda y, x: (y + 1, x))
Y_DOWN = row_pairs(lambda y, x: (y - 1, x))
XH_SWAP = row_pairs(lambda y, x: (y, x + 1))


def prep_kernel(mask_ref, a_ref, out_ref):
    depth, width = a_ref.shape
    part = 128 // CHUNKS
    lane = lax.broadcasted_iota(jnp.int32, (TILE, 128), 1)
    for block in range(width // 128):
        pieces = []
        for t in range(depth // TILE):
            low = mask_ref[t, block * 2]
            high = mask_ref[t, block * 2 + 1]
            keep = jnp.where(lane < TILE, low, high).astype(F32)
            values = a_ref[t * TILE : (t + 1) * TILE, block * 128 : (block + 1) * 128].astype(F32)
            pieces.append(values * keep)
        flipped = jnp.concatenate(pieces, axis=0).T.astype(BF)
        for j in range(CHUNKS):
            out_ref[j, block * part : (block + 1) * part, :] = flipped[j * part : (j + 1) * part, :]


def prep(mask, a):
    depth, width = a.shape
    return pl.pallas_call(
        prep_kernel,
        out_shape=jax.ShapeDtypeStruct((CHUNKS, width // CHUNKS, depth), BF),
        in_specs=[pl.BlockSpec(memory_space=pltpu.SMEM), pl.BlockSpec(memory_space=pltpu.VMEM)],
        out_specs=pl.BlockSpec(memory_space=pltpu.VMEM),
        compiler_params=pltpu.CompilerParams(vmem_limit_bytes=16 * 2**20),
    )(mask, a)


def product_kernel(a_ref, b_ref, out_ref):
    part = 128 // CHUNKS
    rows = a_ref.shape[1]
    step = 256
    for m in range(rows // step):
        total = jnp.dot(a_ref[0, m * step : (m + 1) * step, :], b_ref[...], preferred_element_type=F32).astype(BF)
        for g in range(step // part):
            for e in range(2):
                out_ref[m * (step // part) + g, e, :, :] = total[g * part : (g + 1) * part, e * 128 : (e + 1) * 128]


def product(a_full, b_full, j):
    rows, depth = a_full.shape[1:]
    cols = b_full.shape[1]
    part = 128 // CHUNKS
    return pl.pallas_call(
        product_kernel,
        grid=(cols // 256,),
        out_shape=jax.ShapeDtypeStruct((rows // part, cols // 128, part, 128), BF),
        in_specs=[
            pl.BlockSpec((1, rows, depth), lambda n: (j, 0, 0)),
            pl.BlockSpec((depth, 256), lambda n: (0, n)),
        ],
        out_specs=pl.BlockSpec((rows // part, 2, part, 128), lambda n: (0, n, 0, 0)),
        compiler_params=pltpu.CompilerParams(vmem_limit_bytes=40 * 2**20),
        cost_estimate=pl.CostEstimate(
            flops=2 * rows * depth * cols, bytes_accessed=2 * depth * (rows + cols) + 2 * rows * cols, transcendentals=0
        ),
    )(a_full, b_full)


def finish_kernel(row_gap_ref, gap_ref, *refs):
    directs, mirrors, out_ref = refs[:CHUNKS], refs[CHUNKS : 2 * CHUNKS], refs[-1]
    eye = (
        lax.broadcasted_iota(jnp.int32, (128, 128), 0) == lax.broadcasted_iota(jnp.int32, (128, 128), 1)
    ).astype(BF)
    row_gap = row_gap_ref[...]
    for e in range(directs[0].shape[0]):
        direct = jnp.concatenate([ref[e] for ref in directs], axis=0).astype(F32)
        mirror = jnp.concatenate([ref[e] for ref in mirrors], axis=0)
        flipped = lax.dot_general(eye, mirror, (((1,), (1,)), ((), ())), preferred_element_type=F32)
        span = slice(e * 128, (e + 1) * 128)
        out_ref[:, span] = ((direct + flipped) / (row_gap + gap_ref[:, span])).astype(BF)


def finish(row_gap, gap, directs, mirrors):
    count, part, lanes = directs[0].shape
    rows = part * CHUNKS
    step = 8
    piece = pl.BlockSpec((step, part, lanes), lambda n: (n, 0, 0))
    return pl.pallas_call(
        finish_kernel,
        grid=(count // step,),
        out_shape=jax.ShapeDtypeStruct((rows, count * lanes), BF),
        in_specs=[
            pl.BlockSpec((rows, 1), lambda n: (0, 0)),
            pl.BlockSpec((1, step * lanes), lambda n: (0, n)),
        ]
        + [piece] * (2 * CHUNKS),
        out_specs=pl.BlockSpec((rows, step * lanes), lambda n: (0, n)),
        compiler_params=pltpu.CompilerParams(vmem_limit_bytes=32 * 2**20),
    )(row_gap.reshape(rows, 1), gap.reshape(1, count * lanes), *directs, *mirrors)


def spread(own, swap, up, down, axis, cut):
    half = own.shape[cut] // 2
    far = lax.ppermute(own, axis, swap)
    found = []
    for side, block in ((0, own), (1, far)):
        below = lax.ppermute(block, axis, up)
        above = lax.ppermute(block, axis, down)
        first = lax.ppermute(lax.slice_in_dim(below, 0, half, axis=cut), axis, up)
        second = lax.ppermute(lax.slice_in_dim(above, half, 2 * half, axis=cut), axis, down)
        found += [(0, side, 0, block), (-1, side, 0, below), (1, side, 0, above), (2, side, 0, first), (2, side, half, second)]
    return found


def local(amplitudes, integrals, tile_mask, occ_energy, virt_energy):
    row_place = lax.axis_index("row")
    col_place = lax.axis_index("col")
    local_depth, local_width = amplitudes.shape
    tile_rows = local_depth // TILE
    own_mask = lax.dynamic_slice_in_dim(tile_mask, col_place * tile_rows, tile_rows, 0)
    own = prep(own_mask, amplitudes)
    z, xl, core = col_place // 4, (col_place // 2) % 2, col_place % 2
    y, xh = row_place // 2, row_place % 2

    depth = local_depth * 16
    a_full = jnp.zeros((CHUNKS, local_width // CHUNKS, depth), BF)
    b_full = jnp.zeros((depth, integrals.shape[1]), BF)
    found_a = spread(own, X_SWAP, Z_UP, Z_DOWN, "col", 1)
    found_b = spread(integrals, XH_SWAP, Y_UP, Y_DOWN, "row", 0)
    for offset, side, start, block in found_b:
        place = ((y + offset) % 4) * 2 + (xh + side) % 2
        b_full = lax.dynamic_update_slice(b_full, block, (place * 512 + start, 0))
    for offset, side, start, block in found_a:
        other = lax.ppermute(block, "col", CORE_SWAP)
        for k, piece in ((core, block), (1 - core, other)):
            place = ((z + offset) % 4) * 4 + ((xl + side) % 2) * 2 + k
            a_full = lax.dynamic_update_slice(a_full, piece, (0, start, place * 256))

    directs, mirrors = [], []
    for j in range(CHUNKS):
        made = product(a_full, b_full, j)
        direct = lax.all_to_all(made, "col", split_axis=0, concat_axis=0, tiled=True)
        direct = direct.reshape(128, 128 // CHUNKS, 128)
        directs.append(direct)
        mirrors.append(lax.all_to_all(direct, ("row", "col"), split_axis=0, concat_axis=0, tiled=True))

    gap = (virt_energy[None, :] - occ_energy[:, None]).reshape(-1)
    flat_place = row_place * 16 + col_place
    row_gap = lax.dynamic_slice_in_dim(gap, flat_place * 128, 128, 0)
    return finish(row_gap, gap, directs, mirrors)


def solution(mesh):
    return jax.shard_map(
        local,
        mesh=mesh,
        in_specs=(P("col", "row"), P("row", "col"), P(None, "row"), P(), P()),
        out_specs=P(("row", "col"), None),
        check_vma=False,
    )
```

```python
import functools

import jax
import jax.numpy as jnp
from jax import lax
from jax.experimental import pallas as pl
from jax.experimental.pallas import tpu as pltpu
from jax.sharding import PartitionSpec as P

TILE = 64
CHUNKS = 1
BF = jnp.bfloat16
F32 = jnp.float32


def col_pairs(move):
    pairs = []
    for z in range(4):
        for x in range(2):
            for k in range(2):
                a, b, c = move(z, x, k)
                pairs.append((z * 4 + x * 2 + k, (a % 4) * 4 + (b % 2) * 2 + c % 2))
    return pairs


def row_pairs(move):
    pairs = []
    for y in range(4):
        for x in range(2):
            a, b = move(y, x)
            pairs.append((y * 2 + x, (a % 4) * 2 + b % 2))
    return pairs


Z_UP = col_pairs(lambda z, x, k: (z + 1, x, k))
Z_DOWN = col_pairs(lambda z, x, k: (z - 1, x, k))
X_SWAP = col_pairs(lambda z, x, k: (z, x + 1, k))
CORE_SWAP = col_pairs(lambda z, x, k: (z, x, k + 1))
Y_UP = row_pairs(lambda y, x: (y + 1, x))
Y_DOWN = row_pairs(lambda y, x: (y - 1, x))
XH_SWAP = row_pairs(lambda y, x: (y, x + 1))


def prep_kernel(mask_ref, a_ref, out_ref):
    depth, width = a_ref.shape
    lane = lax.broadcasted_iota(jnp.int32, (TILE, 128), 1)
    half = width // 256
    for block in range(width // 128):
        pieces = []
        for t in range(depth // TILE):
            low = mask_ref[t, block * 2]
            high = mask_ref[t, block * 2 + 1]
            keep = jnp.where(lane < TILE, low, high).astype(F32)
            values = a_ref[t * TILE : (t + 1) * TILE, block * 128 : (block + 1) * 128].astype(F32)
            pieces.append(values * keep)
        row = (block % half) * 128
        out_ref[block // half, row : row + 128, :] = jnp.concatenate(pieces, axis=0).T.astype(BF)


def prep(mask, a):
    depth, width = a.shape
    return pl.pallas_call(
        prep_kernel,
        out_shape=jax.ShapeDtypeStruct((2, width // 2, depth), BF),
        in_specs=[pl.BlockSpec(memory_space=pltpu.SMEM), pl.BlockSpec(memory_space=pltpu.VMEM)],
        out_specs=pl.BlockSpec(memory_space=pltpu.VMEM),
        compiler_params=pltpu.CompilerParams(vmem_limit_bytes=16 * 2**20),
    )(mask, a)


def product_kernel(j, h, taken, *refs):
    a_refs, b_refs = refs[:8], refs[8:16]
    out_ref, a_buf, b_buf, total, taken_buf, out_buf, a_sem, b_sem, t_sem, o_sem = refs[-10:]
    depth, group, wide = 256, 2, 512
    cols = total.shape[1]
    base = 8 * j if taken else 0
    row_place, col_place = lax.axis_index("row"), lax.axis_index("col")
    z, xl = col_place // 4, (col_place // 2) % 2
    y, xh = row_place // 2, row_place % 2

    def a_copy(t):
        at = j if a_refs[t].shape[0] == 2 else 0
        return pltpu.make_async_copy(a_refs[t].at[at], a_buf.at[:, pl.ds(t * depth, depth)], a_sem.at[t])

    def b_copy(src, spot):
        return pltpu.make_async_copy(src, b_buf.at[spot], b_sem.at[spot])

    for t in range(8):
        a_copy(t).start()
        side, offset = t // 4, (0, -1, 1, 2)[t % 4]
        apart = (y + offset - z + 8) % 4
        slot = jnp.where(apart == 1, 2, jnp.where(apart == 2, 3, jnp.where(apart == 3, 1, 0)))
        place = ((xh + xl + side) % 2) * 4 + slot
        b_copy(b_refs[t].at[h if b_refs[t].shape[0] == 2 else 0], place).start()
    if taken:
        pltpu.make_async_copy(refs[16], taken_buf, t_sem).start()
    for t in range(0, 8, group):
        for u in range(t, t + group):
            a_copy(u).wait()
            b_copy(b_refs[0].at[0], u).wait()
        last = t + group == 8
        if last and taken:
            pltpu.make_async_copy(refs[16], taken_buf, t_sem).wait()
        for n in range(cols // wide):
            span = slice(n * wide, (n + 1) * wide)
            deep = b_buf[t : t + group, :, span].reshape(group * depth, wide)
            part = jnp.dot(a_buf[:, t * depth : (t + group) * depth], deep, preferred_element_type=F32)
            if t > 0:
                part = part + total[:, span]
            if not last:
                total[:, span] = part
                continue
            for e in range(wide // 128):
                k = n * (wide // 128) + e
                for g in range(8):
                    piece = part[g * 128 : (g + 1) * 128, e * 128 : (e + 1) * 128]
                    if taken:
                        piece = piece + taken_buf[g, k].astype(F32)
                    out_buf[k, g] = piece.astype(BF)
                pltpu.make_async_copy(out_buf.at[k], out_ref.at[pl.ds(base, 8), k], o_sem.at[k]).start()
    for k in range(cols // 128):
        pltpu.make_async_copy(out_buf.at[k], out_ref.at[pl.ds(base, 8), k], o_sem.at[k]).wait()


def product(a_shards, b_shards, j, h, taken=None, begun=None, also=()):
    rows, depth, cols = 1024, 2048, 1024
    extra = [x for x in (taken, begun) if x is not None] + list(also)
    return pl.pallas_call(
        functools.partial(product_kernel, j, h, taken is not None),
        in_specs=[pl.BlockSpec(memory_space=pl.ANY)] * (16 + len(extra)),
        out_specs=pl.BlockSpec(memory_space=pl.ANY),
        out_shape=jax.ShapeDtypeStruct((8 if taken is None else 16, 8, 128, 128), BF),
        scratch_shapes=[
            pltpu.VMEM((rows, depth), BF),
            pltpu.VMEM((8, 256, cols), BF),
            pltpu.VMEM((rows, cols), F32),
            pltpu.VMEM((8, 8, 128, 128), BF),
            pltpu.VMEM((8, 8, 128, 128), BF),
            pltpu.SemaphoreType.DMA((8,)),
            pltpu.SemaphoreType.DMA((8,)),
            pltpu.SemaphoreType.DMA,
            pltpu.SemaphoreType.DMA((8,)),
        ],
        input_output_aliases={} if begun is None else {17: 0},
        compiler_params=pltpu.CompilerParams(vmem_limit_bytes=60 * 2**20),
        cost_estimate=pl.CostEstimate(
            flops=2 * rows * depth * cols, bytes_accessed=2 * depth * (rows + cols) + 2 * rows * cols, transcendentals=0
        ),
    )(*a_shards, *b_shards, *extra)


def finish_kernel(row_gap_ref, gap_ref, *refs):
    directs, mirrors, out_ref = refs[:CHUNKS], refs[CHUNKS : 2 * CHUNKS], refs[-1]
    eye = (
        lax.broadcasted_iota(jnp.int32, (128, 128), 0) == lax.broadcasted_iota(jnp.int32, (128, 128), 1)
    ).astype(BF)
    row_gap = row_gap_ref[...]
    for e in range(directs[0].shape[0]):
        direct = jnp.concatenate([ref[e] for ref in directs], axis=0).astype(F32)
        mirror = jnp.concatenate([ref[e] for ref in mirrors], axis=0)
        flipped = lax.dot_general(eye, mirror, (((1,), (1,)), ((), ())), preferred_element_type=F32)
        span = slice(e * 128, (e + 1) * 128)
        out_ref[:, span] = ((direct + flipped) / (row_gap + gap_ref[:, span])).astype(BF)


def finish(row_gap, gap, directs, mirrors):
    count, part, lanes = directs[0].shape
    rows = part * CHUNKS
    step = 16
    piece = pl.BlockSpec((step, part, lanes), lambda n: (n, 0, 0))
    return pl.pallas_call(
        finish_kernel,
        grid=(count // step,),
        out_shape=jax.ShapeDtypeStruct((rows, count * lanes), BF),
        in_specs=[
            pl.BlockSpec((rows, 1), lambda n: (0, 0)),
            pl.BlockSpec((1, step * lanes), lambda n: (0, n)),
        ]
        + [piece] * (2 * CHUNKS),
        out_specs=pl.BlockSpec((rows, step * lanes), lambda n: (0, n)),
        compiler_params=pltpu.CompilerParams(vmem_limit_bytes=56 * 2**20),
    )(row_gap.reshape(rows, 1), gap.reshape(1, count * lanes), *directs, *mirrors)


def gate(values, others):
    def body(*refs):
        del refs

    return pl.pallas_call(
        body,
        out_shape=[jax.ShapeDtypeStruct(x.shape, x.dtype) for x in values],
        in_specs=[pl.BlockSpec(memory_space=pl.ANY)] * (len(values) + len(others)),
        out_specs=[pl.BlockSpec(memory_space=pl.ANY)] * len(values),
        input_output_aliases={i: i for i in range(len(values))},
    )(*values, *others)


def local(amplitudes, integrals, tile_mask, occ_energy, virt_energy):
    row_place = lax.axis_index("row")
    col_place = lax.axis_index("col")
    tile_rows = amplitudes.shape[0] // TILE
    move = lambda block, pairs: lax.ppermute(block, "col" if len(pairs) == 16 else "row", pairs)

    core = col_place % 2
    kept = lax.dynamic_slice_in_dim(integrals, core * 256, 256, 0)
    passed = lax.dynamic_slice_in_dim(integrals, (1 - core) * 256, 256, 0)
    b_own = jnp.stack([kept, move(passed, CORE_SWAP)])
    own_mask = lax.dynamic_slice_in_dim(tile_mask, col_place * tile_rows, tile_rows, 0)
    a_own = prep(own_mask, amplitudes)

    a_far = move(a_own, X_SWAP)
    a_below, a_above = move(a_own, Z_UP), move(a_own, Z_DOWN)
    b_below, b_above = move(b_own, Y_UP), move(b_own, Y_DOWN)
    b_first, b_second = move(b_below[:1], Y_UP), move(b_above[1:], Y_DOWN)
    far_below, far_above = move(a_far, Z_UP), move(a_far, Z_DOWN)
    b_far = move(b_own, XH_SWAP)
    b_far_below, b_far_above = move(b_far, Y_UP), move(b_far, Y_DOWN)
    a_below, a_above, far_below, far_above = gate((a_below, a_above, far_below, far_above), (b_far,))
    a_first, a_second = move(a_below[:1], Z_UP), move(a_above[1:], Z_DOWN)
    b_far_first, b_far_second = move(b_first, XH_SWAP), move(b_second, XH_SWAP)
    far_first, far_second = move(far_above[:1], Z_DOWN), move(far_below[1:], Z_UP)
    a_of = lambda j: [
        a_own, a_below, a_above, (a_first, a_second)[j], a_far, far_below, far_above, (far_first, far_second)[j],
    ]
    b_of = lambda h: [
        b_own, b_below, b_above, (b_first, b_second)[h], b_far, b_far_below, b_far_above, (b_far_first, b_far_second)[h],
    ]
    taken = [move(product(a_of(0), b_of(1), 0, 1, also=(b_first,)), CORE_SWAP)]
    taken.append(move(product(a_of(1), b_of(1), 1, 1, also=(b_far_first,)), CORE_SWAP))
    made = product(a_of(0), b_of(0), 0, 0, taken[0])
    made = product(a_of(1), b_of(0), 1, 0, taken[1], made)
    direct = lax.all_to_all(made, "col", split_axis=0, concat_axis=0, tiled=True).reshape(128, 128, 128)
    mirror = lax.all_to_all(direct, ("row", "col"), split_axis=0, concat_axis=0, tiled=True)

    gap = (virt_energy[None, :] - occ_energy[:, None]).reshape(-1)
    flat_place = row_place * 16 + col_place
    row_gap = lax.dynamic_slice_in_dim(gap, flat_place * 128, 128, 0)
    return finish(row_gap, gap, [direct], [mirror])


def solution(mesh):
    return jax.shard_map(
        local,
        mesh=mesh,
        in_specs=(P("col", "row"), P("row", "col"), P(None, "row"), P(), P()),
        out_specs=P(("row", "col"), None),
        check_vma=False,
    )
```

```python
import functools

import jax
import jax.numpy as jnp
from jax import lax
from jax.experimental import pallas as pl
from jax.experimental.pallas import tpu as pltpu
from jax.sharding import PartitionSpec as P

TILE = 64
CHUNKS = 1
BF = jnp.bfloat16
F32 = jnp.float32


def col_pairs(move):
    pairs = []
    for z in range(4):
        for x in range(2):
            for k in range(2):
                a, b, c = move(z, x, k)
                pairs.append((z * 4 + x * 2 + k, (a % 4) * 4 + (b % 2) * 2 + c % 2))
    return pairs


def row_pairs(move):
    pairs = []
    for y in range(4):
        for x in range(2):
            a, b = move(y, x)
            pairs.append((y * 2 + x, (a % 4) * 2 + b % 2))
    return pairs


Z_UP = col_pairs(lambda z, x, k: (z + 1, x, k))
Z_DOWN = col_pairs(lambda z, x, k: (z - 1, x, k))
X_SWAP = col_pairs(lambda z, x, k: (z, x + 1, k))
CORE_SWAP = col_pairs(lambda z, x, k: (z, x, k + 1))
Y_UP = row_pairs(lambda y, x: (y + 1, x))
Y_DOWN = row_pairs(lambda y, x: (y - 1, x))
XH_SWAP = row_pairs(lambda y, x: (y, x + 1))


def prep_kernel(mask_ref, a_ref, out_ref):
    depth, width = a_ref.shape
    lane = lax.broadcasted_iota(jnp.int32, (TILE, 128), 1)
    half = width // 256
    for block in range(width // 128):
        pieces = []
        for t in range(depth // TILE):
            low = mask_ref[t, block * 2]
            high = mask_ref[t, block * 2 + 1]
            keep = jnp.where(lane < TILE, low, high).astype(F32)
            values = a_ref[t * TILE : (t + 1) * TILE, block * 128 : (block + 1) * 128].astype(F32)
            pieces.append(values * keep)
        row = (block % half) * 128
        out_ref[block // half, row : row + 128, :] = jnp.concatenate(pieces, axis=0).T.astype(BF)


def prep(mask, a):
    depth, width = a.shape
    return pl.pallas_call(
        prep_kernel,
        out_shape=jax.ShapeDtypeStruct((2, width // 2, depth), BF),
        in_specs=[pl.BlockSpec(memory_space=pltpu.SMEM), pl.BlockSpec(memory_space=pltpu.VMEM)],
        out_specs=pl.BlockSpec(memory_space=pltpu.VMEM),
        compiler_params=pltpu.CompilerParams(vmem_limit_bytes=16 * 2**20),
    )(mask, a)


def product_kernel(j, h, taken, *refs):
    a_refs, b_refs = refs[:8], refs[8:16]
    out_ref, a_buf, b_buf, total, taken_buf, out_buf, a_sem, b_sem, t_sem, o_sem = refs[-10:]
    depth, group, wide = 256, 2, 512
    cols = total.shape[1]
    base = 8 * j if taken else 0
    row_place, col_place = lax.axis_index("row"), lax.axis_index("col")
    z, xl = col_place // 4, (col_place // 2) % 2
    y, xh = row_place // 2, row_place % 2

    def a_copy(t):
        at = j if a_refs[t].shape[0] == 2 else 0
        return pltpu.make_async_copy(a_refs[t].at[at], a_buf.at[:, pl.ds(t * depth, depth)], a_sem.at[t])

    def b_copy(src, spot):
        return pltpu.make_async_copy(src, b_buf.at[spot], b_sem.at[spot])

    for t in range(8):
        a_copy(t).start()
        side, offset = t // 4, (0, -1, 1, 2)[t % 4]
        apart = (y + offset - z + 8) % 4
        slot = jnp.where(apart == 1, 2, jnp.where(apart == 2, 3, jnp.where(apart == 3, 1, 0)))
        place = ((xh + xl + side) % 2) * 4 + slot
        b_copy(b_refs[t].at[h if b_refs[t].shape[0] == 2 else 0], place).start()
    if taken:
        pltpu.make_async_copy(refs[16], taken_buf, t_sem).start()
    for t in range(0, 8, group):
        for u in range(t, t + group):
            a_copy(u).wait()
            b_copy(b_refs[0].at[0], u).wait()
        last = t + group == 8
        if last and taken:
            pltpu.make_async_copy(refs[16], taken_buf, t_sem).wait()
        for n in range(cols // wide):
            span = slice(n * wide, (n + 1) * wide)
            deep = b_buf[t : t + group, :, span].reshape(group * depth, wide)
            part = jnp.dot(a_buf[:, t * depth : (t + group) * depth], deep, preferred_element_type=F32)
            if t > 0:
                part = part + total[:, span]
            if not last:
                total[:, span] = part
                continue
            for e in range(wide // 128):
                k = n * (wide // 128) + e
                for g in range(8):
                    piece = part[g * 128 : (g + 1) * 128, e * 128 : (e + 1) * 128]
                    if taken:
                        piece = piece + taken_buf[g, k].astype(F32)
                    out_buf[k, g] = piece.astype(BF)
                pltpu.make_async_copy(out_buf.at[k], out_ref.at[pl.ds(base, 8), k], o_sem.at[k]).start()
    for k in range(cols // 128):
        pltpu.make_async_copy(out_buf.at[k], out_ref.at[pl.ds(base, 8), k], o_sem.at[k]).wait()


def product(a_shards, b_shards, j, h, taken=None, begun=None, also=()):
    rows, depth, cols = 1024, 2048, 1024
    extra = [x for x in (taken, begun) if x is not None] + list(also)
    return pl.pallas_call(
        functools.partial(product_kernel, j, h, taken is not None),
        in_specs=[pl.BlockSpec(memory_space=pl.ANY)] * (16 + len(extra)),
        out_specs=pl.BlockSpec(memory_space=pl.ANY),
        out_shape=jax.ShapeDtypeStruct((8 if taken is None else 16, 8, 128, 128), BF),
        scratch_shapes=[
            pltpu.VMEM((rows, depth), BF),
            pltpu.VMEM((8, 256, cols), BF),
            pltpu.VMEM((rows, cols), F32),
            pltpu.VMEM((8, 8, 128, 128), BF),
            pltpu.VMEM((8, 8, 128, 128), BF),
            pltpu.SemaphoreType.DMA((8,)),
            pltpu.SemaphoreType.DMA((8,)),
            pltpu.SemaphoreType.DMA,
            pltpu.SemaphoreType.DMA((8,)),
        ],
        input_output_aliases={} if begun is None else {17: 0},
        compiler_params=pltpu.CompilerParams(vmem_limit_bytes=60 * 2**20),
        cost_estimate=pl.CostEstimate(
            flops=2 * rows * depth * cols, bytes_accessed=2 * depth * (rows + cols) + 2 * rows * cols, transcendentals=0
        ),
    )(*a_shards, *b_shards, *extra)


def finish_kernel(row_gap_ref, gap_ref, *refs):
    directs, mirrors, out_ref = refs[:CHUNKS], refs[CHUNKS : 2 * CHUNKS], refs[-1]
    eye = (
        lax.broadcasted_iota(jnp.int32, (128, 128), 0) == lax.broadcasted_iota(jnp.int32, (128, 128), 1)
    ).astype(BF)
    row_gap = row_gap_ref[...]
    for e in range(directs[0].shape[0]):
        direct = jnp.concatenate([ref[e] for ref in directs], axis=0).astype(F32)
        mirror = jnp.concatenate([ref[e] for ref in mirrors], axis=0)
        flipped = lax.dot_general(eye, mirror, (((1,), (1,)), ((), ())), preferred_element_type=F32)
        span = slice(e * 128, (e + 1) * 128)
        out_ref[:, span] = ((direct + flipped) / (row_gap + gap_ref[:, span])).astype(BF)


def finish(row_gap, gap, directs, mirrors):
    count, part, lanes = directs[0].shape
    rows = part * CHUNKS
    step = 16
    piece = pl.BlockSpec((step, part, lanes), lambda n: (n, 0, 0))
    return pl.pallas_call(
        finish_kernel,
        grid=(count // step,),
        out_shape=jax.ShapeDtypeStruct((rows, count * lanes), BF),
        in_specs=[
            pl.BlockSpec((rows, 1), lambda n: (0, 0)),
            pl.BlockSpec((1, step * lanes), lambda n: (0, n)),
        ]
        + [piece] * (2 * CHUNKS),
        out_specs=pl.BlockSpec((rows, step * lanes), lambda n: (0, n)),
        compiler_params=pltpu.CompilerParams(vmem_limit_bytes=56 * 2**20),
    )(row_gap.reshape(rows, 1), gap.reshape(1, count * lanes), *directs, *mirrors)


def gate(values, others):
    def body(*refs):
        del refs

    return pl.pallas_call(
        body,
        out_shape=[jax.ShapeDtypeStruct(x.shape, x.dtype) for x in values],
        in_specs=[pl.BlockSpec(memory_space=pl.ANY)] * (len(values) + len(others)),
        out_specs=[pl.BlockSpec(memory_space=pl.ANY)] * len(values),
        input_output_aliases={i: i for i in range(len(values))},
    )(*values, *others)


def local(amplitudes, integrals, tile_mask, occ_energy, virt_energy):
    row_place = lax.axis_index("row")
    col_place = lax.axis_index("col")
    tile_rows = amplitudes.shape[0] // TILE
    move = lambda block, pairs: lax.ppermute(block, "col" if len(pairs) == 16 else "row", pairs)

    core = col_place % 2
    kept = lax.dynamic_slice_in_dim(integrals, core * 256, 256, 0)
    passed = lax.dynamic_slice_in_dim(integrals, (1 - core) * 256, 256, 0)
    b_kept, b_other = kept[None], move(passed, CORE_SWAP)[None]
    b_own = jnp.concatenate([b_kept, b_other])
    own_mask = lax.dynamic_slice_in_dim(tile_mask, col_place * tile_rows, tile_rows, 0)
    a_own = prep(own_mask, amplitudes)

    a_far = move(a_own, X_SWAP)
    a_below, a_above = move(a_own, Z_UP), move(a_own, Z_DOWN)
    b_below, b_above = move(b_own, Y_UP), move(b_own, Y_DOWN)
    b_first, b_second = move(b_below[:1], Y_UP), move(b_above[1:], Y_DOWN)
    far_below, far_above = move(a_far, Z_UP), move(a_far, Z_DOWN)
    b_far = [move(x, XH_SWAP) for x in gate((b_kept, b_other), (a_far,))]
    b_far_below, b_far_above = [move(x, Y_UP) for x in b_far], [move(x, Y_DOWN) for x in b_far]
    a_below, a_above, far_below, far_above = gate((a_below, a_above, far_below, far_above), (b_far[1],))
    a_first, a_second = move(a_below[:1], Z_UP), move(a_above[1:], Z_DOWN)
    b_far_first, b_far_second = move(b_first, XH_SWAP), move(b_second, XH_SWAP)
    far_first, far_second = move(far_above[:1], Z_DOWN), move(far_below[1:], Z_UP)
    a_of = lambda j: [
        a_own, a_below, a_above, (a_first, a_second)[j], a_far, far_below, far_above, (far_first, far_second)[j],
    ]
    b_of = lambda h: [
        b_own, b_below, b_above, (b_first, b_second)[h],
        b_far[h], b_far_below[h], b_far_above[h], (b_far_first, b_far_second)[h],
    ]
    taken = [move(product(a_of(0), b_of(1), 0, 1, also=(b_first, b_far[0])), CORE_SWAP)]
    taken.append(move(product(a_of(1), b_of(1), 1, 1, also=(b_far_first, b_far_below[0], b_far_above[0])), CORE_SWAP))
    made = product(a_of(0), b_of(0), 0, 0, taken[0])
    made = product(a_of(1), b_of(0), 1, 0, taken[1], made)
    direct = lax.all_to_all(made, "col", split_axis=0, concat_axis=0, tiled=True).reshape(128, 128, 128)
    mirror = lax.all_to_all(direct, ("row", "col"), split_axis=0, concat_axis=0, tiled=True)

    gap = (virt_energy[None, :] - occ_energy[:, None]).reshape(-1)
    flat_place = row_place * 16 + col_place
    row_gap = lax.dynamic_slice_in_dim(gap, flat_place * 128, 128, 0)
    return finish(row_gap, gap, [direct], [mirror])


def solution(mesh):
    return jax.shard_map(
        local,
        mesh=mesh,
        in_specs=(P("col", "row"), P("row", "col"), P(None, "row"), P(), P()),
        out_specs=P(("row", "col"), None),
        check_vma=False,
    )
```

```python
import functools

import jax
import jax.numpy as jnp
from jax import lax
from jax.experimental import pallas as pl
from jax.experimental.pallas import tpu as pltpu
from jax.sharding import PartitionSpec as P

TILE = 64
BF = jnp.bfloat16
F32 = jnp.float32


def col_pairs(move):
    pairs = []
    for z in range(4):
        for x in range(2):
            for k in range(2):
                a, b, c = move(z, x, k)
                pairs.append((z * 4 + x * 2 + k, (a % 4) * 4 + (b % 2) * 2 + c % 2))
    return pairs


def row_pairs(move):
    pairs = []
    for y in range(4):
        for x in range(2):
            a, b = move(y, x)
            pairs.append((y * 2 + x, (a % 4) * 2 + b % 2))
    return pairs


Z_UP = col_pairs(lambda z, x, k: (z + 1, x, k))
Z_DOWN = col_pairs(lambda z, x, k: (z - 1, x, k))
X_SWAP = col_pairs(lambda z, x, k: (z, x + 1, k))
CORE_SWAP = col_pairs(lambda z, x, k: (z, x, k + 1))
Y_UP = row_pairs(lambda y, x: (y + 1, x))
Y_DOWN = row_pairs(lambda y, x: (y - 1, x))
XH_SWAP = row_pairs(lambda y, x: (y, x + 1))


def prep_kernel(mask_ref, a_ref, out_ref):
    depth, width = a_ref.shape
    lane = lax.broadcasted_iota(jnp.int32, (TILE, 128), 1)
    half = width // 256
    for block in range(width // 128):
        pieces = []
        for t in range(depth // TILE):
            low = mask_ref[t, block * 2]
            high = mask_ref[t, block * 2 + 1]
            keep = jnp.where(lane < TILE, low, high).astype(F32)
            values = a_ref[t * TILE : (t + 1) * TILE, block * 128 : (block + 1) * 128].astype(F32)
            pieces.append(values * keep)
        row = (block % half) * 128
        out_ref[block // half, row : row + 128, :] = jnp.concatenate(pieces, axis=0).T.astype(BF)


def prep(mask, a):
    depth, width = a.shape
    return pl.pallas_call(
        prep_kernel,
        out_shape=jax.ShapeDtypeStruct((2, width // 2, depth), BF),
        in_specs=[pl.BlockSpec(memory_space=pltpu.SMEM), pl.BlockSpec(memory_space=pltpu.VMEM)],
        out_specs=pl.BlockSpec(memory_space=pltpu.VMEM),
        compiler_params=pltpu.CompilerParams(vmem_limit_bytes=16 * 2**20),
    )(mask, a)


def product_kernel(j, h, taken, *refs):
    a_refs, b_refs = refs[:8], refs[8:16]
    out_ref, a_buf, b_buf, total, taken_buf, out_buf, a_sem, b_sem, t_sem, o_sem = refs[-10:]
    depth, group, wide = 256, 2, 512
    cols = total.shape[1]
    base = 8 * j if taken else 0
    row_place, col_place = lax.axis_index("row"), lax.axis_index("col")
    z, xl = col_place // 4, (col_place // 2) % 2
    y, xh = row_place // 2, row_place % 2

    def a_copy(t):
        at = j if a_refs[t].shape[0] == 2 else 0
        return pltpu.make_async_copy(a_refs[t].at[at], a_buf.at[:, pl.ds(t * depth, depth)], a_sem.at[t])

    def b_copy(src, spot):
        return pltpu.make_async_copy(src, b_buf.at[spot], b_sem.at[spot])

    for t in range(8):
        a_copy(t).start()
        side, offset = t // 4, (0, -1, 1, 2)[t % 4]
        apart = (y + offset - z + 8) % 4
        slot = jnp.where(apart == 1, 2, jnp.where(apart == 2, 3, jnp.where(apart == 3, 1, 0)))
        place = ((xh + xl + side) % 2) * 4 + slot
        b_copy(b_refs[t].at[h if b_refs[t].shape[0] == 2 else 0], place).start()
    if taken:
        pltpu.make_async_copy(refs[16], taken_buf, t_sem).start()
    for t in range(0, 8, group):
        for u in range(t, t + group):
            a_copy(u).wait()
            b_copy(b_refs[0].at[0], u).wait()
        last = t + group == 8
        if last and taken:
            pltpu.make_async_copy(refs[16], taken_buf, t_sem).wait()
        for n in range(cols // wide):
            span = slice(n * wide, (n + 1) * wide)
            deep = b_buf[t : t + group, :, span].reshape(group * depth, wide)
            part = jnp.dot(a_buf[:, t * depth : (t + group) * depth], deep, preferred_element_type=F32)
            if t > 0:
                part = part + total[:, span]
            if not last:
                total[:, span] = part
                continue
            for e in range(wide // 128):
                k = n * (wide // 128) + e
                for g in range(8):
                    piece = part[g * 128 : (g + 1) * 128, e * 128 : (e + 1) * 128]
                    if taken:
                        piece = piece + taken_buf[g, k].astype(F32)
                    out_buf[k, g] = piece.astype(BF)
                pltpu.make_async_copy(out_buf.at[k], out_ref.at[pl.ds(base, 8), k], o_sem.at[k]).start()
    for k in range(cols // 128):
        pltpu.make_async_copy(out_buf.at[k], out_ref.at[pl.ds(base, 8), k], o_sem.at[k]).wait()


def product(a_shards, b_shards, j, h, taken=None, begun=None, also=()):
    rows, depth, cols = 1024, 2048, 1024
    extra = [x for x in (taken, begun) if x is not None] + list(also)
    return pl.pallas_call(
        functools.partial(product_kernel, j, h, taken is not None),
        in_specs=[pl.BlockSpec(memory_space=pl.ANY)] * (16 + len(extra)),
        out_specs=pl.BlockSpec(memory_space=pl.ANY),
        out_shape=jax.ShapeDtypeStruct((8 if taken is None else 16, 8, 128, 128), BF),
        scratch_shapes=[
            pltpu.VMEM((rows, depth), BF),
            pltpu.VMEM((8, 256, cols), BF),
            pltpu.VMEM((rows, cols), F32),
            pltpu.VMEM((8, 8, 128, 128), BF),
            pltpu.VMEM((8, 8, 128, 128), BF),
            pltpu.SemaphoreType.DMA((8,)),
            pltpu.SemaphoreType.DMA((8,)),
            pltpu.SemaphoreType.DMA,
            pltpu.SemaphoreType.DMA((8,)),
        ],
        input_output_aliases={} if begun is None else {17: 0},
        compiler_params=pltpu.CompilerParams(vmem_limit_bytes=60 * 2**20),
        cost_estimate=pl.CostEstimate(
            flops=2 * rows * depth * cols, bytes_accessed=2 * depth * (rows + cols) + 2 * rows * cols, transcendentals=0
        ),
    )(*a_shards, *b_shards, *extra)


STEPS = 8


def finish_kernel(row_gap_ref, gap_ref, direct_ref, mirror_ref, out_ref, direct_buf, mirror_buf, out_buf, sems, out_sem):
    eye = (
        lax.broadcasted_iota(jnp.int32, (128, 128), 0) == lax.broadcasted_iota(jnp.int32, (128, 128), 1)
    ).astype(BF)
    step = mirror_ref.shape[0] // STEPS
    row_gap = row_gap_ref[...]

    def take(n, k):
        span = pl.ds(n * step, step)
        src, buf = ((direct_ref, direct_buf), (mirror_ref, mirror_buf))[k]
        return pltpu.make_async_copy(src.at[span], buf.at[span], sems.at[k, n])

    def give(n):
        span = pl.ds(n * step * 128, step * 128)
        return pltpu.make_async_copy(out_buf.at[:, span], out_ref.at[:, span], out_sem.at[n])

    for n in range(STEPS):
        take(n, 0).start()
        take(n, 1).start()
    for n in range(STEPS):
        take(n, 0).wait()
        take(n, 1).wait()
        for e in range(n * step, (n + 1) * step):
            flipped = lax.dot_general(eye, mirror_buf[e], (((1,), (1,)), ((), ())), preferred_element_type=F32)
            span = slice(e * 128, (e + 1) * 128)
            total = direct_buf[e].astype(F32) + flipped
            out_buf[:, span] = (total / (row_gap + gap_ref[:, span])).astype(BF)
        give(n).start()
    for n in range(STEPS):
        give(n).wait()


def finish(row_gap, gap, direct, mirror):
    count, rows, lanes = direct.shape
    vmem, anywhere = pl.BlockSpec(memory_space=pltpu.VMEM), pl.BlockSpec(memory_space=pl.ANY)
    return pl.pallas_call(
        finish_kernel,
        out_shape=jax.ShapeDtypeStruct((rows, count * lanes), BF),
        in_specs=[vmem, vmem, anywhere, anywhere],
        out_specs=anywhere,
        scratch_shapes=[
            pltpu.VMEM(direct.shape, BF),
            pltpu.VMEM(mirror.shape, BF),
            pltpu.VMEM((rows, count * lanes), BF),
            pltpu.SemaphoreType.DMA((2, STEPS)),
            pltpu.SemaphoreType.DMA((STEPS,)),
        ],
        compiler_params=pltpu.CompilerParams(vmem_limit_bytes=58 * 2**20),
    )(row_gap.reshape(rows, 1), gap.reshape(1, count * lanes), direct, mirror)


def gate(values, others):
    def body(*refs):
        del refs

    return pl.pallas_call(
        body,
        out_shape=[jax.ShapeDtypeStruct(x.shape, x.dtype) for x in values],
        in_specs=[pl.BlockSpec(memory_space=pl.ANY)] * (len(values) + len(others)),
        out_specs=[pl.BlockSpec(memory_space=pl.ANY)] * len(values),
        input_output_aliases={i: i for i in range(len(values))},
    )(*values, *others)


def local(amplitudes, integrals, tile_mask, occ_energy, virt_energy):
    row_place = lax.axis_index("row")
    col_place = lax.axis_index("col")
    tile_rows = amplitudes.shape[0] // TILE
    move = lambda block, pairs: lax.ppermute(block, "col" if len(pairs) == 16 else "row", pairs)

    core = col_place % 2
    kept = lax.dynamic_slice_in_dim(integrals, core * 256, 256, 0)
    passed = lax.dynamic_slice_in_dim(integrals, (1 - core) * 256, 256, 0)
    b_kept, b_other = kept[None], move(passed, CORE_SWAP)[None]
    b_own = jnp.concatenate([b_kept, b_other])
    own_mask = lax.dynamic_slice_in_dim(tile_mask, col_place * tile_rows, tile_rows, 0)
    a_own = prep(own_mask, amplitudes)

    a_far = move(a_own, X_SWAP)
    a_below, a_above = move(a_own, Z_UP), move(a_own, Z_DOWN)
    b_below, b_above = move(b_own, Y_UP), move(b_own, Y_DOWN)
    b_first, b_second = move(b_below[:1], Y_UP), move(b_above[1:], Y_DOWN)
    far_below, far_above = move(a_far, Z_UP), move(a_far, Z_DOWN)
    b_far = [move(x, XH_SWAP) for x in gate((b_kept, b_other), (a_far,))]
    b_far_below, b_far_above = [move(x, Y_UP) for x in b_far], [move(x, Y_DOWN) for x in b_far]
    a_below, a_above, far_below, far_above = gate((a_below, a_above, far_below, far_above), (b_far[1],))
    a_first, a_second = move(a_below[:1], Z_UP), move(a_above[1:], Z_DOWN)
    b_far_first, b_far_second = move(b_first, XH_SWAP), move(b_second, XH_SWAP)
    far_first, far_second = move(far_above[:1], Z_DOWN), move(far_below[1:], Z_UP)
    a_of = lambda j: [
        a_own, a_below, a_above, (a_first, a_second)[j], a_far, far_below, far_above, (far_first, far_second)[j],
    ]
    b_of = lambda h: [
        b_own, b_below, b_above, (b_first, b_second)[h],
        b_far[h], b_far_below[h], b_far_above[h], (b_far_first, b_far_second)[h],
    ]
    taken = [move(product(a_of(0), b_of(1), 0, 1, also=(b_first, b_far[0])), CORE_SWAP)]
    taken.append(move(product(a_of(1), b_of(1), 1, 1, also=(b_far_first, b_far_below[0], b_far_above[0])), CORE_SWAP))
    made = product(a_of(0), b_of(0), 0, 0, taken[0])
    made = product(a_of(1), b_of(0), 1, 0, taken[1], made)
    direct = lax.all_to_all(made, "col", split_axis=0, concat_axis=0, tiled=True).reshape(128, 128, 128)
    mirror = lax.all_to_all(direct, ("row", "col"), split_axis=0, concat_axis=0, tiled=True)

    gap = (virt_energy[None, :] - occ_energy[:, None]).reshape(-1)
    flat_place = row_place * 16 + col_place
    row_gap = lax.dynamic_slice_in_dim(gap, flat_place * 128, 128, 0)
    return finish(row_gap, gap, direct, mirror)


def solution(mesh):
    return jax.shard_map(
        local,
        mesh=mesh,
        in_specs=(P("col", "row"), P("row", "col"), P(None, "row"), P(), P()),
        out_specs=P(("row", "col"), None),
        check_vma=False,
    )
```

```python
import functools

import jax
import jax.numpy as jnp
from jax import lax
from jax.experimental import pallas as pl
from jax.experimental.pallas import tpu as pltpu
from jax.sharding import PartitionSpec as P

TILE = 64
BF = jnp.bfloat16
F32 = jnp.float32


def col_pairs(move):
    pairs = []
    for z in range(4):
        for x in range(2):
            for k in range(2):
                a, b, c = move(z, x, k)
                pairs.append((z * 4 + x * 2 + k, (a % 4) * 4 + (b % 2) * 2 + c % 2))
    return pairs


def row_pairs(move):
    pairs = []
    for y in range(4):
        for x in range(2):
            a, b = move(y, x)
            pairs.append((y * 2 + x, (a % 4) * 2 + b % 2))
    return pairs


Z_UP = col_pairs(lambda z, x, k: (z + 1, x, k))
Z_DOWN = col_pairs(lambda z, x, k: (z - 1, x, k))
X_SWAP = col_pairs(lambda z, x, k: (z, x + 1, k))
CORE_SWAP = col_pairs(lambda z, x, k: (z, x, k + 1))
Y_UP = row_pairs(lambda y, x: (y + 1, x))
Y_DOWN = row_pairs(lambda y, x: (y - 1, x))
XH_SWAP = row_pairs(lambda y, x: (y, x + 1))


def prep_kernel(mask_ref, a_ref, out_ref):
    depth, width = a_ref.shape
    lane = lax.broadcasted_iota(jnp.int32, (TILE, 128), 1)
    half = width // 256
    for block in range(width // 128):
        pieces = []
        for t in range(depth // TILE):
            low = mask_ref[t, block * 2]
            high = mask_ref[t, block * 2 + 1]
            keep = jnp.where(lane < TILE, low, high).astype(F32)
            values = a_ref[t * TILE : (t + 1) * TILE, block * 128 : (block + 1) * 128].astype(F32)
            pieces.append(values * keep)
        row = (block % half) * 128
        out_ref[block // half, row : row + 128, :] = jnp.concatenate(pieces, axis=0).T.astype(BF)


def prep(mask, a):
    depth, width = a.shape
    return pl.pallas_call(
        prep_kernel,
        out_shape=jax.ShapeDtypeStruct((2, width // 2, depth), BF),
        in_specs=[pl.BlockSpec(memory_space=pltpu.SMEM), pl.BlockSpec(memory_space=pltpu.VMEM)],
        out_specs=pl.BlockSpec(memory_space=pltpu.VMEM),
        compiler_params=pltpu.CompilerParams(vmem_limit_bytes=16 * 2**20),
    )(mask, a)


def product_kernel(j, h, taken, *refs):
    a_refs, b_refs = refs[:8], refs[8:16]
    out_ref, a_buf, b_buf, total, taken_buf, out_buf, a_sem, b_sem, t_sem, o_sem = refs[-10:]
    depth, group, wide = 256, 2, 512
    cols = total.shape[1]
    base = 8 * j if taken else 0
    row_place, col_place = lax.axis_index("row"), lax.axis_index("col")
    z, xl = col_place // 4, (col_place // 2) % 2
    y, xh = row_place // 2, row_place % 2

    def a_copy(t):
        at = j if a_refs[t].shape[0] == 2 else 0
        return pltpu.make_async_copy(a_refs[t].at[at], a_buf.at[:, pl.ds(t * depth, depth)], a_sem.at[t])

    def b_copy(src, spot):
        return pltpu.make_async_copy(src, b_buf.at[spot], b_sem.at[spot])

    places = []
    for side in range(2):
        for offset in (0, -1, 1, 2):
            apart = (y + offset - z + 8) % 4
            slot = jnp.where(apart == 1, 2, jnp.where(apart == 2, 3, jnp.where(apart == 3, 1, 0)))
            places.append(((xh + xl + side) % 2) * 4 + slot)

    def start_b(t, u):
        pl.when(places[t] == u)(lambda: b_copy(b_refs[t].at[h if b_refs[t].shape[0] == 2 else 0], u).start())

    for u in range(8):
        a_copy(u).start()
        for t in range(8):
            start_b(t, u)
    if taken:
        pltpu.make_async_copy(refs[16], taken_buf, t_sem).start()
    for t in range(0, 8, group):
        for u in range(t, t + group):
            a_copy(u).wait()
            b_copy(b_refs[0].at[0], u).wait()
        last = t + group == 8
        if last and taken:
            pltpu.make_async_copy(refs[16], taken_buf, t_sem).wait()
        for n in range(cols // wide):
            span = slice(n * wide, (n + 1) * wide)
            deep = b_buf[t : t + group, :, span].reshape(group * depth, wide)
            part = jnp.dot(a_buf[:, t * depth : (t + group) * depth], deep, preferred_element_type=F32)
            if t > 0:
                part = part + total[:, span]
            if not last:
                total[:, span] = part
                continue
            for e in range(wide // 128):
                k = n * (wide // 128) + e
                for g in range(8):
                    piece = part[g * 128 : (g + 1) * 128, e * 128 : (e + 1) * 128]
                    if taken:
                        piece = piece + taken_buf[g, k].astype(F32)
                    out_buf[k, g] = piece.astype(BF)
                pltpu.make_async_copy(out_buf.at[k], out_ref.at[pl.ds(base, 8), k], o_sem.at[k]).start()
    for k in range(cols // 128):
        pltpu.make_async_copy(out_buf.at[k], out_ref.at[pl.ds(base, 8), k], o_sem.at[k]).wait()


def product(a_shards, b_shards, j, h, taken=None, begun=None, also=()):
    rows, depth, cols = 1024, 2048, 1024
    extra = [x for x in (taken, begun) if x is not None] + list(also)
    return pl.pallas_call(
        functools.partial(product_kernel, j, h, taken is not None),
        in_specs=[pl.BlockSpec(memory_space=pl.ANY)] * (16 + len(extra)),
        out_specs=pl.BlockSpec(memory_space=pl.ANY),
        out_shape=jax.ShapeDtypeStruct((8 if taken is None else 16, 8, 128, 128), BF),
        scratch_shapes=[
            pltpu.VMEM((rows, depth), BF),
            pltpu.VMEM((8, 256, cols), BF),
            pltpu.VMEM((rows, cols), F32),
            pltpu.VMEM((8, 8, 128, 128), BF),
            pltpu.VMEM((8, 8, 128, 128), BF),
            pltpu.SemaphoreType.DMA((8,)),
            pltpu.SemaphoreType.DMA((8,)),
            pltpu.SemaphoreType.DMA,
            pltpu.SemaphoreType.DMA((8,)),
        ],
        input_output_aliases={} if begun is None else {17: 0},
        compiler_params=pltpu.CompilerParams(vmem_limit_bytes=60 * 2**20),
        cost_estimate=pl.CostEstimate(
            flops=2 * rows * depth * cols, bytes_accessed=2 * depth * (rows + cols) + 2 * rows * cols, transcendentals=0
        ),
    )(*a_shards, *b_shards, *extra)


STEPS = 8


def finish_kernel(row_gap_ref, gap_ref, direct_ref, mirror_ref, out_ref, direct_buf, mirror_buf, out_buf, sems, out_sem):
    eye = (
        lax.broadcasted_iota(jnp.int32, (128, 128), 0) == lax.broadcasted_iota(jnp.int32, (128, 128), 1)
    ).astype(BF)
    step = mirror_ref.shape[0] // STEPS
    row_gap = row_gap_ref[...]

    def take(n, k):
        span = pl.ds(n * step, step)
        src, buf = ((direct_ref, direct_buf), (mirror_ref, mirror_buf))[k]
        return pltpu.make_async_copy(src.at[span], buf.at[span], sems.at[k, n])

    def give(n):
        span = pl.ds(n * step * 128, step * 128)
        return pltpu.make_async_copy(out_buf.at[:, span], out_ref.at[:, span], out_sem.at[n])

    for n in range(STEPS):
        take(n, 0).start()
        take(n, 1).start()
    for n in range(STEPS):
        take(n, 0).wait()
        take(n, 1).wait()
        for e in range(n * step, (n + 1) * step):
            flipped = lax.dot_general(eye, mirror_buf[e], (((1,), (1,)), ((), ())), preferred_element_type=F32)
            span = slice(e * 128, (e + 1) * 128)
            total = direct_buf[e].astype(F32) + flipped
            out_buf[:, span] = (total / (row_gap + gap_ref[:, span])).astype(BF)
        give(n).start()
    for n in range(STEPS):
        give(n).wait()


def finish(row_gap, gap, direct, mirror):
    count, rows, lanes = direct.shape
    vmem, anywhere = pl.BlockSpec(memory_space=pltpu.VMEM), pl.BlockSpec(memory_space=pl.ANY)
    return pl.pallas_call(
        finish_kernel,
        out_shape=jax.ShapeDtypeStruct((rows, count * lanes), BF),
        in_specs=[vmem, vmem, anywhere, anywhere],
        out_specs=anywhere,
        scratch_shapes=[
            pltpu.VMEM(direct.shape, BF),
            pltpu.VMEM(mirror.shape, BF),
            pltpu.VMEM((rows, count * lanes), BF),
            pltpu.SemaphoreType.DMA((2, STEPS)),
            pltpu.SemaphoreType.DMA((STEPS,)),
        ],
        compiler_params=pltpu.CompilerParams(vmem_limit_bytes=58 * 2**20),
    )(row_gap.reshape(rows, 1), gap.reshape(1, count * lanes), direct, mirror)


def gate(values, others):
    def body(*refs):
        del refs

    return pl.pallas_call(
        body,
        out_shape=[jax.ShapeDtypeStruct(x.shape, x.dtype) for x in values],
        in_specs=[pl.BlockSpec(memory_space=pl.ANY)] * (len(values) + len(others)),
        out_specs=[pl.BlockSpec(memory_space=pl.ANY)] * len(values),
        input_output_aliases={i: i for i in range(len(values))},
    )(*values, *others)


def local(amplitudes, integrals, tile_mask, occ_energy, virt_energy):
    row_place = lax.axis_index("row")
    col_place = lax.axis_index("col")
    tile_rows = amplitudes.shape[0] // TILE
    move = lambda block, pairs: lax.ppermute(block, "col" if len(pairs) == 16 else "row", pairs)

    core = col_place % 2
    kept = lax.dynamic_slice_in_dim(integrals, core * 256, 256, 0)
    passed = lax.dynamic_slice_in_dim(integrals, (1 - core) * 256, 256, 0)
    b_kept, b_other = kept[None], move(passed, CORE_SWAP)[None]
    b_own = jnp.concatenate([b_kept, b_other])
    own_mask = lax.dynamic_slice_in_dim(tile_mask, col_place * tile_rows, tile_rows, 0)
    a_own = prep(own_mask, amplitudes)

    a_far = move(a_own, X_SWAP)
    a_below, a_above = move(a_own, Z_UP), move(a_own, Z_DOWN)
    b_below, b_above = move(b_own, Y_UP), move(b_own, Y_DOWN)
    b_first, b_second = move(b_below[:1], Y_UP), move(b_above[1:], Y_DOWN)
    far_below, far_above = move(a_far, Z_UP), move(a_far, Z_DOWN)
    b_far = [move(x, XH_SWAP) for x in gate((b_kept, b_other), (a_far,))]
    b_far_below, b_far_above = [move(x, Y_UP) for x in b_far], [move(x, Y_DOWN) for x in b_far]
    a_below, a_above, far_below, far_above = gate((a_below, a_above, far_below, far_above), (b_far[1],))
    a_first, a_second = move(a_below[:1], Z_UP), move(a_above[1:], Z_DOWN)
    b_far_first, b_far_second = move(b_first, XH_SWAP), move(b_second, XH_SWAP)
    far_first, far_second = move(far_above[:1], Z_DOWN), move(far_below[1:], Z_UP)
    a_of = lambda j: [
        a_own, a_below, a_above, (a_first, a_second)[j], a_far, far_below, far_above, (far_first, far_second)[j],
    ]
    b_of = lambda h: [
        b_own, b_below, b_above, (b_first, b_second)[h],
        b_far[h], b_far_below[h], b_far_above[h], (b_far_first, b_far_second)[h],
    ]
    taken = [move(product(a_of(0), b_of(1), 0, 1, also=(b_first, b_far[0])), CORE_SWAP)]
    taken.append(move(product(a_of(1), b_of(1), 1, 1, also=(b_far_first, b_far_below[0], b_far_above[0])), CORE_SWAP))
    made = product(a_of(0), b_of(0), 0, 0, taken[0])
    made = product(a_of(1), b_of(0), 1, 0, taken[1], made)
    direct = lax.all_to_all(made, "col", split_axis=0, concat_axis=0, tiled=True).reshape(128, 128, 128)
    mirror = lax.all_to_all(direct, ("row", "col"), split_axis=0, concat_axis=0, tiled=True)

    gap = (virt_energy[None, :] - occ_energy[:, None]).reshape(-1)
    flat_place = row_place * 16 + col_place
    row_gap = lax.dynamic_slice_in_dim(gap, flat_place * 128, 128, 0)
    return finish(row_gap, gap, direct, mirror)


def solution(mesh):
    return jax.shard_map(
        local,
        mesh=mesh,
        in_specs=(P("col", "row"), P("row", "col"), P(None, "row"), P(), P()),
        out_specs=P(("row", "col"), None),
        check_vma=False,
    )
```

```python
import functools

import jax
import jax.numpy as jnp
from jax import lax
from jax.experimental import pallas as pl
from jax.experimental.pallas import tpu as pltpu
from jax.sharding import PartitionSpec as P

TILE = 64
BF = jnp.bfloat16
F32 = jnp.float32


def col_pairs(move):
    pairs = []
    for z in range(4):
        for x in range(2):
            for k in range(2):
                a, b, c = move(z, x, k)
                pairs.append((z * 4 + x * 2 + k, (a % 4) * 4 + (b % 2) * 2 + c % 2))
    return pairs


def row_pairs(move):
    pairs = []
    for y in range(4):
        for x in range(2):
            a, b = move(y, x)
            pairs.append((y * 2 + x, (a % 4) * 2 + b % 2))
    return pairs


Z_UP = col_pairs(lambda z, x, k: (z + 1, x, k))
Z_DOWN = col_pairs(lambda z, x, k: (z - 1, x, k))
X_SWAP = col_pairs(lambda z, x, k: (z, x + 1, k))
CORE_SWAP = col_pairs(lambda z, x, k: (z, x, k + 1))
Y_UP = row_pairs(lambda y, x: (y + 1, x))
Y_DOWN = row_pairs(lambda y, x: (y - 1, x))
XH_SWAP = row_pairs(lambda y, x: (y, x + 1))


def prep_kernel(mask_ref, a_ref, out_ref):
    depth, width = a_ref.shape
    lane = lax.broadcasted_iota(jnp.int32, (TILE, 128), 1)
    half = width // 256
    for block in range(width // 128):
        pieces = []
        for t in range(depth // TILE):
            low = mask_ref[t, block * 2]
            high = mask_ref[t, block * 2 + 1]
            keep = jnp.where(lane < TILE, low, high).astype(F32)
            values = a_ref[t * TILE : (t + 1) * TILE, block * 128 : (block + 1) * 128].astype(F32)
            pieces.append(values * keep)
        row = (block % half) * 128
        out_ref[block // half, row : row + 128, :] = jnp.concatenate(pieces, axis=0).T.astype(BF)


def prep(mask, a):
    depth, width = a.shape
    return pl.pallas_call(
        prep_kernel,
        out_shape=jax.ShapeDtypeStruct((2, width // 2, depth), BF),
        in_specs=[pl.BlockSpec(memory_space=pltpu.SMEM), pl.BlockSpec(memory_space=pltpu.VMEM)],
        out_specs=pl.BlockSpec(memory_space=pltpu.VMEM),
        compiler_params=pltpu.CompilerParams(vmem_limit_bytes=16 * 2**20),
    )(mask, a)


def product_kernel(j, h, taken, *refs):
    a_refs, b_refs = refs[:8], refs[8:16]
    out_ref, a_buf, b_buf, total, taken_buf, out_buf, a_sem, b_sem, t_sem, o_sem = refs[-10:]
    depth, wide = 256, 512
    cols = total.shape[1]
    base = 8 * j if taken else 0
    row_place, col_place = lax.axis_index("row"), lax.axis_index("col")
    z, xl = col_place // 4, (col_place // 2) % 2
    y, xh = row_place // 2, row_place % 2

    def a_copy(t):
        at = j if a_refs[t].shape[0] == 2 else 0
        return pltpu.make_async_copy(a_refs[t].at[at], a_buf.at[:, pl.ds(t * depth, depth)], a_sem.at[t])

    def b_copy(src, spot):
        return pltpu.make_async_copy(src, b_buf.at[spot], b_sem.at[spot])

    places = []
    for side in range(2):
        for offset in (0, -1, 1, 2):
            apart = (y + offset - z + 8) % 4
            slot = jnp.where(apart == 1, 2, jnp.where(apart == 2, 3, jnp.where(apart == 3, 1, 0)))
            places.append(((xh + xl + side) % 2) * 4 + slot)

    def start_b(t, u):
        pl.when(places[t] == u)(lambda: b_copy(b_refs[t].at[h if b_refs[t].shape[0] == 2 else 0], u).start())

    for u in range(8):
        a_copy(u).start()
        for t in range(8):
            start_b(t, u)
    if taken:
        pltpu.make_async_copy(refs[16], taken_buf, t_sem).start()
    for t, group in ((0, 1), (1, 1), (2, 2), (4, 2), (6, 2)):
        for u in range(t, t + group):
            a_copy(u).wait()
            b_copy(b_refs[0].at[0], u).wait()
        last = t + group == 8
        if last and taken:
            pltpu.make_async_copy(refs[16], taken_buf, t_sem).wait()
        for n in range(cols // wide):
            span = slice(n * wide, (n + 1) * wide)
            deep = b_buf[t : t + group, :, span].reshape(group * depth, wide)
            part = jnp.dot(a_buf[:, t * depth : (t + group) * depth], deep, preferred_element_type=F32)
            if t > 0:
                part = part + total[:, span]
            if not last:
                total[:, span] = part
                continue
            for e in range(wide // 128):
                k = n * (wide // 128) + e
                for g in range(8):
                    piece = part[g * 128 : (g + 1) * 128, e * 128 : (e + 1) * 128]
                    if taken:
                        piece = piece + taken_buf[g, k].astype(F32)
                    out_buf[k, g] = piece.astype(BF)
                pltpu.make_async_copy(out_buf.at[k], out_ref.at[pl.ds(base, 8), k], o_sem.at[k]).start()
    for k in range(cols // 128):
        pltpu.make_async_copy(out_buf.at[k], out_ref.at[pl.ds(base, 8), k], o_sem.at[k]).wait()


def product(a_shards, b_shards, j, h, taken=None, begun=None, also=()):
    rows, depth, cols = 1024, 2048, 1024
    extra = [x for x in (taken, begun) if x is not None] + list(also)
    return pl.pallas_call(
        functools.partial(product_kernel, j, h, taken is not None),
        in_specs=[pl.BlockSpec(memory_space=pl.ANY)] * (16 + len(extra)),
        out_specs=pl.BlockSpec(memory_space=pl.ANY),
        out_shape=jax.ShapeDtypeStruct((8 if taken is None else 16, 8, 128, 128), BF),
        scratch_shapes=[
            pltpu.VMEM((rows, depth), BF),
            pltpu.VMEM((8, 256, cols), BF),
            pltpu.VMEM((rows, cols), F32),
            pltpu.VMEM((8, 8, 128, 128), BF),
            pltpu.VMEM((8, 8, 128, 128), BF),
            pltpu.SemaphoreType.DMA((8,)),
            pltpu.SemaphoreType.DMA((8,)),
            pltpu.SemaphoreType.DMA,
            pltpu.SemaphoreType.DMA((8,)),
        ],
        input_output_aliases={} if begun is None else {17: 0},
        compiler_params=pltpu.CompilerParams(vmem_limit_bytes=60 * 2**20),
        cost_estimate=pl.CostEstimate(
            flops=2 * rows * depth * cols, bytes_accessed=2 * depth * (rows + cols) + 2 * rows * cols, transcendentals=0
        ),
    )(*a_shards, *b_shards, *extra)


STEPS = 16


def finish_kernel(row_gap_ref, gap_ref, direct_ref, mirror_ref, out_ref, direct_buf, mirror_buf, out_buf, sems, out_sem):
    eye = (
        lax.broadcasted_iota(jnp.int32, (128, 128), 0) == lax.broadcasted_iota(jnp.int32, (128, 128), 1)
    ).astype(BF)
    step = mirror_ref.shape[0] // STEPS
    row_gap = row_gap_ref[...]

    def take(n, k):
        span = pl.ds(n * step, step)
        src, buf = ((direct_ref, direct_buf), (mirror_ref, mirror_buf))[k]
        return pltpu.make_async_copy(src.at[span], buf.at[span], sems.at[k, n])

    def give(n):
        span = pl.ds(n * step * 128, step * 128)
        return pltpu.make_async_copy(out_buf.at[:, span], out_ref.at[:, span], out_sem.at[n])

    for n in range(STEPS):
        take(n, 0).start()
        take(n, 1).start()
    for n in range(STEPS):
        take(n, 0).wait()
        take(n, 1).wait()
        for e in range(n * step, (n + 1) * step):
            flipped = lax.dot_general(eye, mirror_buf[e], (((1,), (1,)), ((), ())), preferred_element_type=F32)
            span = slice(e * 128, (e + 1) * 128)
            total = direct_buf[e].astype(F32) + flipped
            out_buf[:, span] = (total / (row_gap + gap_ref[:, span])).astype(BF)
        give(n).start()
    for n in range(STEPS):
        give(n).wait()


def finish(row_gap, gap, direct, mirror):
    count, rows, lanes = direct.shape
    vmem, anywhere = pl.BlockSpec(memory_space=pltpu.VMEM), pl.BlockSpec(memory_space=pl.ANY)
    return pl.pallas_call(
        finish_kernel,
        out_shape=jax.ShapeDtypeStruct((rows, count * lanes), BF),
        in_specs=[vmem, vmem, anywhere, anywhere],
        out_specs=anywhere,
        scratch_shapes=[
            pltpu.VMEM(direct.shape, BF),
            pltpu.VMEM(mirror.shape, BF),
            pltpu.VMEM((rows, count * lanes), BF),
            pltpu.SemaphoreType.DMA((2, STEPS)),
            pltpu.SemaphoreType.DMA((STEPS,)),
        ],
        compiler_params=pltpu.CompilerParams(vmem_limit_bytes=58 * 2**20),
    )(row_gap.reshape(rows, 1), gap.reshape(1, count * lanes), direct, mirror)


def gate(values, others):
    def body(*refs):
        del refs

    return pl.pallas_call(
        body,
        out_shape=[jax.ShapeDtypeStruct(x.shape, x.dtype) for x in values],
        in_specs=[pl.BlockSpec(memory_space=pl.ANY)] * (len(values) + len(others)),
        out_specs=[pl.BlockSpec(memory_space=pl.ANY)] * len(values),
        input_output_aliases={i: i for i in range(len(values))},
    )(*values, *others)


def local(amplitudes, integrals, tile_mask, occ_energy, virt_energy):
    row_place = lax.axis_index("row")
    col_place = lax.axis_index("col")
    tile_rows = amplitudes.shape[0] // TILE
    move = lambda block, pairs: lax.ppermute(block, "col" if len(pairs) == 16 else "row", pairs)

    core = col_place % 2
    kept = lax.dynamic_slice_in_dim(integrals, core * 256, 256, 0)
    passed = lax.dynamic_slice_in_dim(integrals, (1 - core) * 256, 256, 0)
    b_kept, b_other = kept[None], move(passed, CORE_SWAP)[None]
    b_own = jnp.concatenate([b_kept, b_other])
    own_mask = lax.dynamic_slice_in_dim(tile_mask, col_place * tile_rows, tile_rows, 0)
    a_own = prep(own_mask, amplitudes)

    a_far = move(a_own, X_SWAP)
    a_below, a_above = move(a_own, Z_UP), move(a_own, Z_DOWN)
    b_below, b_above = move(b_own, Y_UP), move(b_own, Y_DOWN)
    b_first, b_second = move(b_below[:1], Y_UP), move(b_above[1:], Y_DOWN)
    far_below, far_above = move(a_far, Z_UP), move(a_far, Z_DOWN)
    b_far = [move(x, XH_SWAP) for x in gate((b_kept, b_other), (a_far,))]
    b_far_below, b_far_above = [move(x, Y_UP) for x in b_far], [move(x, Y_DOWN) for x in b_far]
    a_below, a_above, far_below, far_above = gate((a_below, a_above, far_below, far_above), (b_far[1],))
    a_first, a_second = move(a_below[:1], Z_UP), move(a_above[1:], Z_DOWN)
    b_far_first, b_far_second = move(b_first, XH_SWAP), move(b_second, XH_SWAP)
    far_first, far_second = move(far_above[:1], Z_DOWN), move(far_below[1:], Z_UP)
    a_of = lambda j: [
        a_own, a_below, a_above, (a_first, a_second)[j], a_far, far_below, far_above, (far_first, far_second)[j],
    ]
    b_of = lambda h: [
        b_own, b_below, b_above, (b_first, b_second)[h],
        b_far[h], b_far_below[h], b_far_above[h], (b_far_first, b_far_second)[h],
    ]
    taken = [move(product(a_of(0), b_of(1), 0, 1, also=(b_first, b_far[0])), CORE_SWAP)]
    taken.append(move(product(a_of(1), b_of(1), 1, 1, also=(b_far_first, b_far_below[0], b_far_above[0])), CORE_SWAP))
    made = product(a_of(0), b_of(0), 0, 0, taken[0])
    made = product(a_of(1), b_of(0), 1, 0, taken[1], made)
    direct = lax.all_to_all(made, "col", split_axis=0, concat_axis=0, tiled=True).reshape(128, 128, 128)
    mirror = lax.all_to_all(direct, ("row", "col"), split_axis=0, concat_axis=0, tiled=True)

    gap = (virt_energy[None, :] - occ_energy[:, None]).reshape(-1)
    flat_place = row_place * 16 + col_place
    row_gap = lax.dynamic_slice_in_dim(gap, flat_place * 128, 128, 0)
    return finish(row_gap, gap, direct, mirror)


def solution(mesh):
    return jax.shard_map(
        local,
        mesh=mesh,
        in_specs=(P("col", "row"), P("row", "col"), P(None, "row"), P(), P()),
        out_specs=P(("row", "col"), None),
        check_vma=False,
    )
```
